32 devices in a mesh: groups: 2 (over y), dp: 16 (over z, x, core).
Axes of the slice: x: 2, y: 2, z: 4, core: 2. Of those that a mesh axis runs over, the one named last changes fastest.
Arguments:
- tokens: bfloat16 [8192, 8192], P(('groups', 'dp')), parts along dimension 0, may hold values from -6 to 6
- base_weight: bfloat16 [8192, 256], replicated, may hold values from -0.0625 to 0.0625
- panels: bfloat16 [64, 540672], P('groups', 'dp'), parts along dimension 0
- upstream: bfloat16 [8192, 256], P(('groups', 'dp')), parts along dimension 0, may hold values from -0.59765625 to 0.59765625
- seq_slot: int32 [128], P('groups'), parts along dimension 0, may hold values from 0 to 3, as said below
- device_jobs: int32 [32, 4], P('groups'), parts along dimension 0, may hold values from -1 to 31, as said below
Outputs:
- projected: bfloat16 [8192, 256], P(('groups', 'dp')), parts along dimension 0
- grads: bfloat16 [64, 540672], P('groups', 'dp'), parts along dimension 0
The draws below stay inside these ranges and needn't reach their ends.
There are 2 independent parts, one for each index of `groups`. The reference program is written for one: setup_inputs(seed, part) draws one part's arguments, and reference() takes and returns one part's arrays. A program takes and returns all parts, laid end to end along the dimension named above; an argument that names none is the same for every part. Nothing has to cross between parts.
Inputs may be any that keep to these rules, and one draw needn't show every extreme that they name: `device_jobs`: row e lists the distinct jobs of device e's slots, live entries first and -1 in the unused slots after them; every row has one live slot or more, and at least one row uses all 4. `seq_slot`: each sequence names a live slot of its device's row in device_jobs, and every live slot is named by at least one sequence of that device.
All inputs are finite; a program needn't handle non-finite values.
Results may differ from the reference program's by a relative error of at most 0.0049.
Values may be sent and summed in bfloat16 or wider, within the bound.
A program may use at most 128 MiB of HBM per device.

```python
import jax
import jax.numpy as jnp
from jax import lax

D = 8192
HEAD_FEATURES = 256
RANK = 64
SLOTS = 4
DEVICE_SEQUENCES = 4
SEQUENCE_TOKENS = 64
TOKENS = 4096
JOBS = 32
PANEL = 8448
N_DP = 16


def job_layout(key):
    keys = jax.random.split(key, 6)
    raw = jax.random.randint(keys[0], (N_DP,), 0, JOBS)
    start = raw * raw // JOBS * raw // JOBS
    devices = jnp.arange(N_DP)
    top_device = jax.random.randint(keys[1], (), 0, N_DP)
    start = jnp.where(devices == top_device, JOBS - 1, start)
    live = jax.random.randint(keys[2], (N_DP,), 1, SLOTS + 1)
    full_device = jax.random.randint(keys[3], (), 0, N_DP)
    live = jnp.where(devices == full_device, SLOTS, live)
    slot_pos = jnp.arange(SLOTS)
    jobs = jnp.where(slot_pos[None, :] < live[:, None], (start[:, None] + slot_pos[None, :]) % JOBS, -1)
    seq_pos = jnp.arange(DEVICE_SEQUENCES)
    extra = jax.random.randint(keys[4], (N_DP, DEVICE_SEQUENCES), 0, 1 << 20) % live[:, None]
    drawn = jnp.where(seq_pos[None, :] < live[:, None], seq_pos[None, :], extra)
    row_keys = jax.random.split(keys[5], N_DP)
    shuffled = jax.vmap(jax.random.permutation)(row_keys, drawn)
    return (jobs.astype(jnp.int32), shuffled.reshape(-1).astype(jnp.int32))


def draw_device_jobs(key, part):
    jobs, slots = job_layout(key)
    return jobs


def draw_seq_slot(key, part):
    jobs, slots = job_layout(key)
    return slots


def draw_panels(key, part):
    key = jax.random.fold_in(key, 11)
    values = jax.random.normal(key, (JOBS, PANEL, RANK), jnp.float32)
    row_scale = jnp.where(jnp.arange(PANEL) < D, D ** (-0.5), RANK ** (-0.5)).astype(jnp.float32)
    values = values * row_scale[None, :, None]
    return values.reshape(JOBS, PANEL * RANK).astype(jnp.bfloat16)


def block_scale(rng, shape, cuts, least, top_value):
    factor_of, own = 1.0, jax.random.fold_in(rng, 6)
    for dim, parts in cuts:
        heights = jnp.exp(jax.random.uniform(jax.random.fold_in(own, dim), (parts,), jnp.float32, least / len(cuts), top_value / len(cuts)))
        factor_of = factor_of * jnp.repeat(heights, shape[dim] // parts).reshape([-1 if axis == dim else 1 for axis in range(len(shape))])
    return factor_of


def gaussian(key, extent, scale, most, shards=(), dtype=jnp.bfloat16):
    values = jax.random.normal(key, extent, jnp.float32) * scale
    if len(shards) > 0:
        values = block_scale(key, extent, shards, -0.22, 0.18) * values
    return jnp.clip(values, min=-most, max=most).astype(dtype)


def setup_inputs(seed: int = 0, part: int = 0) -> dict:
    key_of = jax.random.split(jax.random.key(seed), 7)
    part_keys = jax.random.split(jax.random.fold_in(key_of[6], part), 7)
    return {
        "tokens": gaussian(part_keys[0], (TOKENS, D), 1.0, 6.0, ((0, 16),)),
        "base_weight": gaussian(key_of[1], (D, HEAD_FEATURES), D ** -0.5, 0.0625),
        "panels": draw_panels(jax.random.fold_in(jax.random.fold_in(key_of[6], part), 71), part),
        "upstream": gaussian(part_keys[3], (TOKENS, HEAD_FEATURES), 0.1, 0.59765625, ((0, 16),)),
        "seq_slot": draw_seq_slot(jax.random.fold_in(jax.random.fold_in(key_of[6], part), 71), part),
        "device_jobs": draw_device_jobs(jax.random.fold_in(jax.random.fold_in(key_of[6], part), 71), part),
    }


adapter_scale = 0.5


def reference(tokens, base_weight, panels, upstream, seq_slot, device_jobs):
    frozen_output = jnp.dot(tokens, base_weight, preferred_element_type=jnp.float32)
    owner = (jnp.arange(N_DP * DEVICE_SEQUENCES) // DEVICE_SEQUENCES).astype(jnp.int32)
    job_ids = device_jobs[owner, seq_slot].astype(jnp.int32)
    sequence_token_rows = tokens.reshape(N_DP * DEVICE_SEQUENCES, SEQUENCE_TOKENS, D)
    seq_grads = upstream.reshape(N_DP * DEVICE_SEQUENCES, SEQUENCE_TOKENS, HEAD_FEATURES)

    def step(total_sums, item):
        x_seq, dy_seq, job_now = item
        job_now = job_now.astype(jnp.int32)
        panel = lax.dynamic_index_in_dim(panels, job_now, 0, keepdims=False).reshape(PANEL, RANK)
        adapter_down_rows = panel[:D]
        bt_rows = panel[D:]
        lowrank = jnp.dot(x_seq, adapter_down_rows, preferred_element_type=jnp.float32).astype(jnp.bfloat16)
        adapted_output = jnp.dot(lowrank, bt_rows.T, preferred_element_type=jnp.float32)
        back_rank = jnp.dot(dy_seq, bt_rows, preferred_element_type=jnp.float32).astype(jnp.bfloat16)
        grad_a = jnp.dot(x_seq.T, back_rank, preferred_element_type=jnp.float32)
        grad_b = jnp.dot(dy_seq.T, lowrank, preferred_element_type=jnp.float32)
        term = jnp.concatenate([grad_a, grad_b], axis=0).reshape(1, PANEL * RANK)
        before = lax.dynamic_slice_in_dim(total_sums, job_now, 1, 0)
        total_sums = lax.dynamic_update_slice_in_dim(total_sums, before + term, job_now, 0)
        return total_sums, adapted_output

    start = jnp.zeros((JOBS, PANEL * RANK), jnp.float32)
    total_sums, adapted_output = lax.scan(step, start, (sequence_token_rows, seq_grads, job_ids))
    projected = (frozen_output + adapter_scale * adapted_output.reshape(N_DP * DEVICE_SEQUENCES * SEQUENCE_TOKENS, HEAD_FEATURES)).astype(jnp.bfloat16)
    grads = (adapter_scale * total_sums).astype(jnp.bfloat16)
    return projected, grads
```

```python
import functools

import jax
import jax.numpy as jnp
from jax import lax
from jax.experimental import pallas as pl
from jax.experimental.pallas import tpu as pltpu
from jax.sharding import PartitionSpec as P

RANK = 64
CHUNKS = 2

adapter_scale = 0.5


def flip_kernel(tokens_ref, upstream_ref, *out_refs):
    width = tokens_ref.shape[1]
    step = upstream_ref.shape[1]
    part = out_refs[0].shape[1]

    @pl.loop(0, width // step)
    def _(i):
        turned = tokens_ref[:, pl.ds(pl.multiple_of(i * step, step), step)].T
        for h, out_ref in enumerate(out_refs):
            out_ref[pl.ds(pl.multiple_of(i * step, step), step), :] = turned[:, h * part : (h + 1) * part]

    turned = upstream_ref[...].T
    for h, out_ref in enumerate(out_refs):
        out_ref[pl.ds(width, step), :] = turned[:, h * part : (h + 1) * part]


def flip(tokens, upstream):
    count, width = tokens.shape
    head = upstream.shape[1]
    part = count // CHUNKS
    shape = jax.ShapeDtypeStruct((width + head, part), tokens.dtype)
    vmem = pl.BlockSpec(memory_space=pltpu.VMEM)
    return pl.pallas_call(
        flip_kernel,
        out_shape=[shape] * CHUNKS,
        in_specs=[vmem, vmem],
        out_specs=[vmem] * CHUNKS,
        compiler_params=pltpu.CompilerParams(vmem_limit_bytes=40 * 2**20),
        name="flip",
    )(tokens, upstream)


def partial_kernel(slot_count, jobs_ref, cols_ref, slot_ref, down_ref, out_ref):
    source = pl.program_id(0)
    factor = jnp.concatenate(
        [down_ref[jobs_ref[source * slot_count + s]] for s in range(slot_count)], axis=0
    )
    product = jnp.dot(factor, cols_ref[0], preferred_element_type=jnp.float32)
    slot = slot_ref[0]
    total = jnp.zeros(out_ref.shape[1:], jnp.float32)
    for s in range(slot_count):
        total += jnp.where(slot == s, product[s * RANK : (s + 1) * RANK], 0.0)
    out_ref[0] = total.astype(out_ref.dtype)


def partial_lowrank(jobs, cols, slot, down_t, slot_count):
    count, row_count, part = cols.shape
    return pl.pallas_call(
        functools.partial(partial_kernel, slot_count),
        out_shape=jax.ShapeDtypeStruct((count, RANK, part), jnp.float32),
        grid_spec=pltpu.PrefetchScalarGridSpec(
            num_scalar_prefetch=1,
            grid=(count,),
            in_specs=[
                pl.BlockSpec((1, row_count, part), lambda e, jobs: (e, 0, 0)),
                pl.BlockSpec((1, 1, part), lambda e, jobs: (e, 0, 0)),
                pl.BlockSpec(down_t.shape, lambda e, jobs: (0, 0, 0)),
            ],
            out_specs=pl.BlockSpec((1, RANK, part), lambda e, jobs: (e, 0, 0)),
        ),
        compiler_params=pltpu.CompilerParams(vmem_limit_bytes=40 * 2**20),
        cost_estimate=pl.CostEstimate(
            flops=2 * count * row_count * part * RANK * slot_count, bytes_accessed=cols.size * 2, transcendentals=0
        ),
        name="partial_lowrank",
    )(jobs, cols, slot, down_t)


def grads_kernel(slot_count, width, *refs):
    jobs_ref, first_ref = refs[:2]
    cols_refs = refs[2 : 2 + CHUNKS]
    slot_refs = refs[2 + CHUNKS : 2 + 2 * CHUNKS]
    right_refs = refs[2 + 2 * CHUNKS : 2 + 4 * CHUNKS]
    out_ref, sums = refs[2 + 4 * CHUNKS :]
    source = pl.program_id(0)
    row_count = cols_refs[0].shape[1]
    job_total = out_ref.shape[0]

    @pl.when(source == 0)
    def _():
        sums[...] = jnp.zeros_like(sums)

    def term(right_of):
        total = None
        for h in range(CHUNKS):
            slot = slot_refs[h][0]
            right = right_refs[right_of * CHUNKS + h][0]
            spread = jnp.concatenate(
                [jnp.where(slot == s, right, jnp.zeros_like(right)) for s in range(slot_count)], axis=0
            )
            product = lax.dot_general(
                cols_refs[h][0], spread, (((1,), (1,)), ((), ())), preferred_element_type=jnp.float32
            )
            total = product if total is None else total + product
        return total

    row = first_ref[0] + lax.broadcasted_iota(jnp.int32, (row_count, 1), 0)
    total = jnp.where(row < width, term(0), term(1))
    for s in range(slot_count):
        job = jobs_ref[source * slot_count + s]
        at = pl.ds(pl.multiple_of(job * row_count, 2), row_count)
        sums[at, :] += total[:, s * RANK : (s + 1) * RANK]

    @pl.when(source == pl.num_programs(0) - 1)
    def _():
        @pl.loop(0, row_count // 2)
        def _(pair):
            even = sums[pl.ds(2 * pair, job_total, stride=row_count), :]
            odd = sums[pl.ds(2 * pair + 1, job_total, stride=row_count), :]
            both = jnp.concatenate([even, odd], axis=1) * adapter_scale
            out_ref[:, pl.ds(pl.multiple_of(pair * 2 * RANK, 2 * RANK), 2 * RANK)] = both.astype(out_ref.dtype)


def all_grads(jobs, first_row, cols, slots, back, low, job_total, width, slot_count):
    count, row_count, part = cols[0].shape
    block = lambda rows: pl.BlockSpec((1, rows, part), lambda e, jobs, first: (e, 0, 0))
    return pl.pallas_call(
        functools.partial(grads_kernel, slot_count, width),
        out_shape=jax.ShapeDtypeStruct((job_total, row_count * RANK), jnp.bfloat16),
        grid_spec=pltpu.PrefetchScalarGridSpec(
            num_scalar_prefetch=2,
            grid=(count,),
            in_specs=[block(row_count)] * CHUNKS + [block(1)] * CHUNKS + [block(RANK)] * (2 * CHUNKS),
            out_specs=pl.BlockSpec((job_total, row_count * RANK), lambda e, jobs, first: (0, 0)),
            scratch_shapes=[pltpu.VMEM((job_total * row_count, RANK), jnp.float32)],
        ),
        compiler_params=pltpu.CompilerParams(vmem_limit_bytes=48 * 2**20),
        name="grads",
    )(jobs, first_row, *cols, *slots, *back, *low)


def slot_ups(panels, jobs, first_row, width, head):
    count, slot_count = jobs.shape
    job_total = panels.shape[0]
    row_count = panels.shape[1] // RANK
    kept = min(row_count, head)
    start = jnp.clip(width - first_row, 0, row_count - kept)
    rows = lax.dynamic_slice_in_dim(panels, start * RANK, kept * RANK, axis=1)
    place = first_row + start - width
    if kept < head:
        wide = jnp.pad(rows, ((0, 0), (head * RANK, head * RANK)))
        rows = lax.dynamic_slice_in_dim(
            wide, jnp.clip(head - place, 0, head + kept) * RANK, head * RANK, axis=1
        )
        live = place > -kept
    else:
        live = place >= 0
    rows = jnp.where(live, rows, jnp.zeros_like(rows))
    chosen = rows[jobs.reshape(-1)]
    mine = lax.psum_scatter(chosen, "dp", scatter_dimension=0, tiled=True)
    return mine.reshape(slot_count, head, RANK)


def local(tokens, base_weight, panels, upstream, seq_slot, device_jobs):
    count = lax.axis_size("dp")
    device = lax.axis_index("dp")
    width = tokens.shape[1]
    head = base_weight.shape[1]
    slot_count = device_jobs.shape[1]
    seq_count = seq_slot.shape[0] // count
    seq_len = tokens.shape[0] // seq_count
    job_total = panels.shape[0]
    row_count = panels.shape[1] // RANK
    part = tokens.shape[0] // CHUNKS
    first_row = device * row_count
    jobs = jnp.maximum(device_jobs, 0)
    flat_jobs = jobs.reshape(-1)

    sent = flip(tokens, upstream)
    cols = [
        lax.all_to_all(x.reshape(count, row_count, part), "dp", split_axis=0, concat_axis=0, tiled=True)
        for x in sent
    ]

    token_slot = jnp.repeat(seq_slot, seq_len).reshape(count, 1, CHUNKS, part)
    slots = [token_slot[:, :, h] for h in range(CHUNKS)]

    frozen_output = jnp.dot(tokens, base_weight, preferred_element_type=jnp.float32)
    down_t = panels.reshape(job_total, row_count, RANK).transpose(0, 2, 1)
    row_index = first_row + jnp.arange(row_count)
    down_t = jnp.where((row_index < width)[None, None, :], down_t, jnp.zeros_like(down_t))

    bt_rows = slot_ups(panels, jobs, first_row, width, head)
    my_slots = lax.dynamic_slice_in_dim(seq_slot, device * seq_count, seq_count)
    seq_bt = bt_rows[my_slots]
    seq_grads = upstream.reshape(seq_count, seq_len, head)
    back_rank = jnp.einsum(
        "slh,shr->rsl", seq_grads, seq_bt, preferred_element_type=jnp.float32
    ).astype(jnp.bfloat16)
    back_all = lax.all_gather(back_rank.reshape(RANK, CHUNKS * part), "dp", axis=0)
    back = [back_all[:, :, h * part : (h + 1) * part] for h in range(CHUNKS)]

    low, mine = [], []
    for h in range(CHUNKS):
        partial = partial_lowrank(flat_jobs, cols[h], slots[h], down_t, slot_count)
        own = lax.psum_scatter(partial, "dp", scatter_dimension=0).astype(jnp.bfloat16)
        mine.append(own)
        low.append(lax.all_gather(own, "dp", axis=0))

    grads = all_grads(
        flat_jobs, first_row.reshape(1), cols, slots, back, low, job_total, width, slot_count
    )
    lowrank = jnp.concatenate(mine, axis=1).reshape(RANK, seq_count, seq_len)
    adapted = jnp.einsum("rsl,shr->slh", lowrank, seq_bt, preferred_element_type=jnp.float32)
    projected = (frozen_output + adapter_scale * adapted.reshape(-1, head)).astype(jnp.bfloat16)
    return projected, grads


def solution(mesh):
    in_specs = (
        P(("groups", "dp"), None),
        P(),
        P("groups", "dp"),
        P(("groups", "dp"), None),
        P("groups"),
        P("groups", None),
    )
    out_specs = (P(("groups", "dp"), None), P("groups", "dp"))
    return jax.shard_map(local, mesh=mesh, in_specs=in_specs, out_specs=out_specs, check_vma=False)
```

```python
import functools

import jax
import jax.numpy as jnp
from jax import lax
from jax.experimental import pallas as pl
from jax.experimental.pallas import tpu as pltpu
from jax.sharding import PartitionSpec as P

RANK = 64


adapter_scale = 0.5


def slot_panels(panels, device_jobs, rank_size):
    count = lax.axis_size("dp")
    slot_count = device_jobs.shape[1]
    chosen = jnp.take(panels, jnp.maximum(device_jobs, 0).reshape(-1), axis=0)
    outgoing = chosen.reshape(count, slot_count, panels.shape[1])
    arrived = lax.all_to_all(outgoing, "dp", split_axis=0, concat_axis=2, tiled=True)
    return arrived.reshape(slot_count, -1, rank_size)


def plain_local(tokens, base_weight, panels, upstream, seq_slot, device_jobs):
    count = lax.axis_size("dp")
    device = lax.axis_index("dp")
    width = tokens.shape[1]
    head_columns = base_weight.shape[1]
    rank_size = RANK
    seq_count = seq_slot.shape[0] // count
    seq_len = tokens.shape[0] // seq_count
    row_count = panels.shape[1] // rank_size
    job_total = panels.shape[0]
    my_slots = lax.dynamic_slice_in_dim(seq_slot, device * seq_count, seq_count)
    stacked = slot_panels(panels, device_jobs, rank_size)
    frozen_output = jnp.dot(tokens, base_weight, preferred_element_type=jnp.float32)
    seq_panels = jnp.take(stacked, my_slots, axis=0)
    adapter_down_rows = seq_panels[:, :width]
    bt_rows = seq_panels[:, width:]
    sequence_token_rows = tokens.reshape(seq_count, seq_len, width)
    seq_grads = upstream.reshape(seq_count, seq_len, head_columns)
    lowrank = jnp.einsum(
        "ovc,ocm->ovm", sequence_token_rows, adapter_down_rows, preferred_element_type=jnp.float32
    ).astype(jnp.bfloat16)
    adapted_output = jnp.einsum(
        "slr,shr->slh", lowrank, bt_rows, preferred_element_type=jnp.float32
    )
    projected = (frozen_output + adapter_scale * adapted_output.reshape(-1, head_columns)).astype(
        jnp.bfloat16
    )
    back_rank = jnp.einsum(
        "slh,shr->slr", seq_grads, bt_rows, preferred_element_type=jnp.float32
    ).astype(jnp.bfloat16)
    left = jnp.concatenate([tokens, upstream], axis=1)
    left_cols = lax.all_to_all(left, "dp", split_axis=1, concat_axis=0, tiled=True)
    right = jnp.concatenate([back_rank, lowrank], axis=2).reshape(-1, 2 * rank_size)
    right_all = lax.all_gather(right, "dp", axis=0, tiled=True)
    source = jnp.arange(count * seq_count) // seq_count
    owners = device_jobs[source, seq_slot]
    owners = jnp.where(owners < 0, job_total, owners)
    group = 16
    turns = count // group
    block_seqs = group * seq_count
    left_blocks = left_cols.reshape(turns, block_seqs, seq_len, row_count)
    right_blocks = right_all.reshape(turns, block_seqs, seq_len, 2 * rank_size)
    owner_blocks = owners.reshape(turns, block_seqs)
    first_row = device * row_count
    last_row = first_row + row_count - 1
    straddles = jnp.logical_and(first_row < width, last_row >= width)
    all_up = first_row >= width
    row_index = first_row + jnp.arange(row_count)
    down_rows = (row_index < width)[None, :, None]
    job_index = jnp.arange(job_total)

    def one_half(left_seq, right_seq):
        factor = jnp.where(all_up, right_seq[:, :, rank_size:], right_seq[:, :, :rank_size])
        return jnp.einsum("nlp,nlr->npr", left_seq, factor, preferred_element_type=jnp.float32)

    def two_halves(left_seq, right_seq):
        down_term = jnp.einsum(
            "nlp,nlr->npr",
            left_seq,
            right_seq[:, :, :rank_size],
            preferred_element_type=jnp.float32,
        )
        up_term = jnp.einsum(
            "nlp,nlr->npr",
            left_seq,
            right_seq[:, :, rank_size:],
            preferred_element_type=jnp.float32,
        )
        return jnp.where(down_rows, down_term, up_term)

    def accumulate(total_sums, item):
        left_seq, right_seq, owner_now = item
        term = lax.cond(straddles, two_halves, one_half, left_seq, right_seq)
        selector = (owner_now[:, None] == job_index[None, :]).astype(jnp.float32)
        added = jnp.dot(
            selector.T,
            term.reshape(block_seqs, -1),
            preferred_element_type=jnp.float32,
            precision=lax.Precision.HIGHEST,
        )
        return (total_sums + added, None)

    start = jnp.zeros((job_total, row_count * rank_size), jnp.float32)
    summed_output, unused = lax.scan(accumulate, start, (left_blocks, right_blocks, owner_blocks))
    grads = (adapter_scale * summed_output).astype(jnp.bfloat16)
    return (projected, grads)


def flip_kernel(tokens_ref, upstream_ref, out_ref):
    width = tokens_ref.shape[1]
    step = upstream_ref.shape[1]

    @pl.loop(0, width // step)
    def _(i):
        at = pl.ds(pl.multiple_of(i * step, step), step)
        out_ref[at, :] = tokens_ref[:, at].T

    out_ref[pl.ds(width, step), :] = upstream_ref[...].T


def flip(tokens, upstream):
    count, width = tokens.shape
    vmem = pl.BlockSpec(memory_space=pltpu.VMEM)
    return pl.pallas_call(
        flip_kernel,
        out_shape=jax.ShapeDtypeStruct((width + upstream.shape[1], count), tokens.dtype),
        in_specs=[vmem, vmem],
        out_specs=vmem,
        compiler_params=pltpu.CompilerParams(vmem_limit_bytes=40 * 2**20),
        name="flip",
    )(tokens, upstream)


def pick_slots(product, slot, slot_count):
    total = jnp.zeros((RANK, product.shape[1]), jnp.float32)
    for s in range(slot_count):
        total += jnp.where(slot == s, product[s * RANK : (s + 1) * RANK], 0.0)
    return total


def exchange_kernel(
    owner,
    jobs_ref,
    sent_ref,
    tokens_ref,
    weight_ref,
    up_ref,
    down_ref,
    slot_ref,
    job_ref,
    projected_ref,
    grads_ref,
    cols,
    tokens,
    weight,
    bt,
    up_t,
    back,
    part_out,
    part_in,
    low,
    sums,
    frozen,
    cols_send,
    cols_recv,
    bt_send,
    bt_recv,
    back_send,
    back_recv,
    part_send,
    part_recv,
    low_send,
    low_recv,
    local_sem,
):
    count, row_count, tokens_here = cols.shape
    slot_count = bt.shape[0] // RANK
    width = tokens.shape[1]
    job_total = grads_ref.shape[0]
    half = job_total // 2
    up_start = width - owner * row_count
    up_count = row_count - up_start
    me = lax.axis_index("dp")

    def peer(k):
        return lax.rem(me + k, count)

    def cols_copy(dest):
        return pltpu.make_async_remote_copy(
            src_ref=sent_ref.at[pl.ds(pl.multiple_of(dest * row_count, 16), row_count)],
            dst_ref=cols.at[me],
            send_sem=cols_send.at[dest],
            recv_sem=cols_recv.at[me],
            device_id={"dp": dest},
            device_id_type=pl.DeviceIdType.MESH,
        )

    def bt_copy(dest):
        return pltpu.make_async_remote_copy(
            src_ref=up_ref.at[dest],
            dst_ref=bt,
            send_sem=bt_send.at[dest],
            recv_sem=bt_recv,
            device_id={"dp": dest},
            device_id_type=pl.DeviceIdType.MESH,
        )

    def back_copy(dest):
        return pltpu.make_async_remote_copy(
            src_ref=back.at[me],
            dst_ref=back.at[me],
            send_sem=back_send.at[dest],
            recv_sem=back_recv.at[me],
            device_id={"dp": dest},
            device_id_type=pl.DeviceIdType.MESH,
        )

    def part_copy(dest):
        return pltpu.make_async_remote_copy(
            src_ref=part_out.at[dest],
            dst_ref=part_in.at[me],
            send_sem=part_send.at[dest],
            recv_sem=part_recv.at[me],
            device_id={"dp": dest},
            device_id_type=pl.DeviceIdType.MESH,
        )

    def low_copy():
        return pltpu.make_async_remote_copy(
            src_ref=low.at[me],
            dst_ref=low.at[me],
            send_sem=low_send,
            recv_sem=low_recv.at[me],
            device_id={"dp": owner},
            device_id_type=pl.DeviceIdType.MESH,
        )

    def arrival(buffer, sem):
        return pltpu.make_async_copy(buffer, buffer, sem)

    tokens_in = pltpu.make_async_copy(tokens_ref, tokens, local_sem.at[0])
    weight_in = pltpu.make_async_copy(weight_ref, weight, local_sem.at[1])
    own_in = pltpu.make_async_copy(
        sent_ref.at[pl.ds(pl.multiple_of(me * row_count, 16), row_count)], cols.at[me], local_sem.at[2]
    )
    up_in = pltpu.make_async_copy(sent_ref.at[pl.ds(width, up_count)], up_t, local_sem.at[3])
    bt_in = pltpu.make_async_copy(up_ref.at[me], bt, local_sem.at[4])

    barrier = pltpu.get_barrier_semaphore()

    @pl.loop(1, count)
    def _(k):
        pl.semaphore_signal(barrier, inc=1, device_id={"dp": peer(k)}, device_id_type=pl.DeviceIdType.MESH)

    tokens_in.start()
    weight_in.start()
    own_in.start()
    up_in.start()
    pl.semaphore_wait(barrier, count - 1)

    @pl.when(me == owner)
    def _():
        bt_in.start()

        @pl.loop(1, count)
        def _(k):
            bt_copy(peer(k)).start()

    @pl.loop(1, count)
    def _(k):
        cols_copy(peer(k)).start()

    sums[...] = jnp.zeros_like(sums)
    frozen[...] = jnp.zeros_like(frozen)
    tokens_in.wait()
    weight_in.wait()
    depth = width // 8

    @pl.loop(0, 8)
    def _(i):
        at = pl.ds(pl.multiple_of(i * depth, depth), depth)
        frozen[...] += jnp.dot(tokens[:, at], weight[at, :], preferred_element_type=jnp.float32)

    own_in.wait()
    up_in.wait()

    @pl.when(me == owner)
    def _():
        bt_in.wait()

    @pl.when(me != owner)
    def _():
        arrival(bt, bt_recv).wait()

    my_slot = slot_ref[me]
    back[me] = pick_slots(
        jnp.dot(bt[...], up_t[...], preferred_element_type=jnp.float32), my_slot, slot_count
    ).astype(back.dtype)

    @pl.loop(1, count)
    def _(k):
        back_copy(peer(k)).start()

    def lowrank_part(source):
        factor = jnp.concatenate(
            [down_ref[jobs_ref[source * slot_count + s]] for s in range(slot_count)], axis=0
        )
        product = jnp.dot(factor, cols[source], preferred_element_type=jnp.float32)
        return pick_slots(product, slot_ref[source], slot_count)

    def add_grads(source, right, first, rows):
        job = job_ref[source]

        @pl.loop(0, half // 2)
        def _(i):
            pieces = []
            for pair in range(2):
                for upper in range(2):
                    here = job == 2 * i + pair + upper * half
                    pieces.append(jnp.where(here, right, jnp.zeros_like(right)))
            product = lax.dot_general(
                cols[source, pl.ds(first, rows)],
                jnp.concatenate(pieces, axis=0),
                (((1,), (1,)), ((), ())),
                preferred_element_type=jnp.float32,
            )
            for pair in range(2):
                at = pl.ds(pl.multiple_of((2 * i + pair) * row_count + first, 8), rows)
                sums[at, :] += product[:, pair * 2 * RANK : (pair + 1) * 2 * RANK]

    own_part = lowrank_part(me)
    part_in[me] = own_part.astype(part_in.dtype)
    add_grads(me, back[me], 0, row_count)

    @pl.loop(1, count)
    def _(k):
        source = lax.rem(me - k + count, count)
        arrival(cols.at[source], cols_recv.at[source]).wait()
        part_out[source] = lowrank_part(source).astype(part_out.dtype)
        part_copy(source).start()
        arrival(back.at[source], back_recv.at[source]).wait()
        add_grads(source, back[source], 0, row_count)

    total = own_part
    for k in range(1, count):
        source = lax.rem(me - k + count, count)
        arrival(part_in.at[source], part_recv.at[source]).wait()
        total += part_in[source].astype(jnp.float32)
    mine = total.astype(low.dtype)
    low[me] = mine

    @pl.when(me != owner)
    def _():
        low_copy().start()

    spread = jnp.concatenate(
        [jnp.where(my_slot == s, mine, jnp.zeros_like(mine)) for s in range(slot_count)], axis=0
    )
    adapted = jnp.dot(spread.T, bt[...], preferred_element_type=jnp.float32)
    projected_ref[...] = (frozen[...] + adapter_scale * adapted).astype(projected_ref.dtype)

    @pl.when(me == owner)
    def _():
        @pl.loop(0, half)
        def _(i):
            at = pl.ds(pl.multiple_of(i * row_count + up_start, 8), up_count)
            sums[at, :] = jnp.zeros((up_count, 2 * RANK), jnp.float32)

        add_grads(me, low[me], up_start, up_count)

        @pl.loop(1, count)
        def _(k):
            source = lax.rem(me - k + count, count)
            arrival(low.at[source], low_recv.at[source]).wait()
            add_grads(source, low[source], up_start, up_count)

    @pl.loop(0, row_count // 2)
    def _(pair):
        even = sums[pl.ds(2 * pair, half, stride=row_count), :]
        odd = sums[pl.ds(2 * pair + 1, half, stride=row_count), :]
        first = jnp.concatenate([even[:, :RANK], odd[:, :RANK]], axis=1)
        second = jnp.concatenate([even[:, RANK:], odd[:, RANK:]], axis=1)
        both = jnp.concatenate([first, second], axis=0) * adapter_scale
        grads_ref[:, pl.ds(pl.multiple_of(pair * 2 * RANK, 2 * RANK), 2 * RANK)] = both.astype(
            grads_ref.dtype
        )

    @pl.when(me == owner)
    def _():
        @pl.loop(1, count)
        def _(k):
            bt_copy(peer(k)).wait_send()

    @pl.when(me != owner)
    def _():
        low_copy().wait_send()

    @pl.loop(1, count)
    def _(k):
        cols_copy(peer(k)).wait_send()
        back_copy(peer(k)).wait_send()
        part_copy(peer(k)).wait_send()


def local(tokens, base_weight, panels, upstream, seq_slot, device_jobs):
    count = lax.axis_size("dp")
    device = lax.axis_index("dp")
    tokens_here, width = tokens.shape
    head = base_weight.shape[1]
    slot_count = device_jobs.shape[1]
    seq_count = seq_slot.shape[0] // count
    seq_len = tokens_here // seq_count
    job_total = panels.shape[0]
    row_count = panels.shape[1] // RANK
    owner = count - 1
    up_start = width - owner * row_count
    bf16 = jnp.bfloat16
    jobs = jnp.maximum(device_jobs, 0)

    sent = flip(tokens, upstream)
    rows_t = panels.reshape(job_total, row_count, RANK).transpose(0, 2, 1)
    up_t = rows_t[:, :, up_start:][jobs].reshape(count, slot_count * RANK, head)
    row_index = device * row_count + jnp.arange(row_count)
    down_t = jnp.where((row_index < width)[None, None, :], rows_t, jnp.zeros_like(rows_t))
    token_slot = jnp.repeat(seq_slot, seq_len).reshape(count, 1, tokens_here)
    seq_job = jobs[jnp.arange(count * seq_count) // seq_count, seq_slot]
    token_job = jnp.repeat(seq_job, seq_len).reshape(count, 1, tokens_here)

    vmem = pl.BlockSpec(memory_space=pltpu.VMEM)
    hbm = pl.BlockSpec(memory_space=pl.ANY)
    dma = pltpu.SemaphoreType.DMA
    return pl.pallas_call(
        functools.partial(exchange_kernel, owner),
        out_shape=(
            jax.ShapeDtypeStruct((tokens_here, head), bf16),
            jax.ShapeDtypeStruct((job_total, row_count * RANK), bf16),
        ),
        in_specs=[pl.BlockSpec(memory_space=pltpu.SMEM), hbm, hbm, hbm, hbm, vmem, vmem, vmem],
        out_specs=(vmem, vmem),
        scratch_shapes=[
            pltpu.VMEM((count, row_count, tokens_here), bf16),
            pltpu.VMEM((tokens_here, width), bf16),
            pltpu.VMEM((width, head), bf16),
            pltpu.VMEM((slot_count * RANK, head), bf16),
            pltpu.VMEM((head, tokens_here), bf16),
            pltpu.VMEM((count, RANK, tokens_here), bf16),
            pltpu.VMEM((count, RANK, tokens_here), bf16),
            pltpu.VMEM((count, RANK, tokens_here), bf16),
            pltpu.VMEM((count, RANK, tokens_here), bf16),
            pltpu.VMEM((job_total // 2 * row_count, 2 * RANK), jnp.float32),
            pltpu.VMEM((tokens_here, head), jnp.float32),
            dma((count,)),
            dma((count,)),
            dma((count,)),
            dma,
            dma((count,)),
            dma((count,)),
            dma((count,)),
            dma((count,)),
            dma,
            dma((count,)),
            dma((5,)),
        ],
        compiler_params=pltpu.CompilerParams(
            collective_id=0, has_side_effects=True, vmem_limit_bytes=56 * 2**20
        ),
        name="exchange",
    )(jobs.reshape(-1), sent, tokens, base_weight, up_t, down_t, token_slot, token_job)


def solution(mesh):
    in_specs = (
        P(("groups", "dp"), None),
        P(),
        P("groups", "dp"),
        P(("groups", "dp"), None),
        P("groups"),
        P("groups", None),
    )
    out_specs = (P(("groups", "dp"), None), P("groups", "dp"))

    def chosen(tokens, base_weight, panels, upstream, seq_slot, device_jobs):
        width, head = base_weight.shape
        row_count = (width + head) // lax.axis_size("dp")
        fits = row_count >= head and row_count % 16 == 0 and panels.shape[0] % 32 == 0
        body = local if fits else plain_local
        return body(tokens, base_weight, panels, upstream, seq_slot, device_jobs)

    return jax.shard_map(chosen, mesh=mesh, in_specs=in_specs, out_specs=out_specs, check_vma=False)
```

```python
import functools

import jax
import jax.numpy as jnp
from jax import lax
from jax.experimental import pallas as pl
from jax.experimental.pallas import tpu as pltpu
from jax.sharding import PartitionSpec as P

RANK = 64


adapter_scale = 0.5


def slot_panels(panels, device_jobs, rank_size):
    count = lax.axis_size("dp")
    slot_count = device_jobs.shape[1]
    chosen = jnp.take(panels, jnp.maximum(device_jobs, 0).reshape(-1), axis=0)
    outgoing = chosen.reshape(count, slot_count, panels.shape[1])
    arrived = lax.all_to_all(outgoing, "dp", split_axis=0, concat_axis=2, tiled=True)
    return arrived.reshape(slot_count, -1, rank_size)


def plain_local(tokens, base_weight, panels, upstream, seq_slot, device_jobs):
    count = lax.axis_size("dp")
    device = lax.axis_index("dp")
    width = tokens.shape[1]
    head_columns = base_weight.shape[1]
    rank_size = RANK
    seq_count = seq_slot.shape[0] // count
    seq_len = tokens.shape[0] // seq_count
    row_count = panels.shape[1] // rank_size
    job_total = panels.shape[0]
    my_slots = lax.dynamic_slice_in_dim(seq_slot, device * seq_count, seq_count)
    stacked = slot_panels(panels, device_jobs, rank_size)
    frozen_output = jnp.dot(tokens, base_weight, preferred_element_type=jnp.float32)
    seq_panels = jnp.take(stacked, my_slots, axis=0)
    adapter_down_rows = seq_panels[:, :width]
    bt_rows = seq_panels[:, width:]
    sequence_token_rows = tokens.reshape(seq_count, seq_len, width)
    seq_grads = upstream.reshape(seq_count, seq_len, head_columns)
    lowrank = jnp.einsum(
        "ovc,ocm->ovm", sequence_token_rows, adapter_down_rows, preferred_element_type=jnp.float32
    ).astype(jnp.bfloat16)
    adapted_output = jnp.einsum(
        "slr,shr->slh", lowrank, bt_rows, preferred_element_type=jnp.float32
    )
    projected = (frozen_output + adapter_scale * adapted_output.reshape(-1, head_columns)).astype(
        jnp.bfloat16
    )
    back_rank = jnp.einsum(
        "slh,shr->slr", seq_grads, bt_rows, preferred_element_type=jnp.float32
    ).astype(jnp.bfloat16)
    left = jnp.concatenate([tokens, upstream], axis=1)
    left_cols = lax.all_to_all(left, "dp", split_axis=1, concat_axis=0, tiled=True)
    right = jnp.concatenate([back_rank, lowrank], axis=2).reshape(-1, 2 * rank_size)
    right_all = lax.all_gather(right, "dp", axis=0, tiled=True)
    source = jnp.arange(count * seq_count) // seq_count
    owners = device_jobs[source, seq_slot]
    owners = jnp.where(owners < 0, job_total, owners)
    group = 16
    turns = count // group
    block_seqs = group * seq_count
    left_blocks = left_cols.reshape(turns, block_seqs, seq_len, row_count)
    right_blocks = right_all.reshape(turns, block_seqs, seq_len, 2 * rank_size)
    owner_blocks = owners.reshape(turns, block_seqs)
    first_row = device * row_count
    last_row = first_row + row_count - 1
    straddles = jnp.logical_and(first_row < width, last_row >= width)
    all_up = first_row >= width
    row_index = first_row + jnp.arange(row_count)
    down_rows = (row_index < width)[None, :, None]
    job_index = jnp.arange(job_total)

    def one_half(left_seq, right_seq):
        factor = jnp.where(all_up, right_seq[:, :, rank_size:], right_seq[:, :, :rank_size])
        return jnp.einsum("nlp,nlr->npr", left_seq, factor, preferred_element_type=jnp.float32)

    def two_halves(left_seq, right_seq):
        down_term = jnp.einsum(
            "nlp,nlr->npr",
            left_seq,
            right_seq[:, :, :rank_size],
            preferred_element_type=jnp.float32,
        )
        up_term = jnp.einsum(
            "nlp,nlr->npr",
            left_seq,
            right_seq[:, :, rank_size:],
            preferred_element_type=jnp.float32,
        )
        return jnp.where(down_rows, down_term, up_term)

    def accumulate(total_sums, item):
        left_seq, right_seq, owner_now = item
        term = lax.cond(straddles, two_halves, one_half, left_seq, right_seq)
        selector = (owner_now[:, None] == job_index[None, :]).astype(jnp.float32)
        added = jnp.dot(
            selector.T,
            term.reshape(block_seqs, -1),
            preferred_element_type=jnp.float32,
            precision=lax.Precision.HIGHEST,
        )
        return (total_sums + added, None)

    start = jnp.zeros((job_total, row_count * rank_size), jnp.float32)
    summed_output, unused = lax.scan(accumulate, start, (left_blocks, right_blocks, owner_blocks))
    grads = (adapter_scale * summed_output).astype(jnp.bfloat16)
    return (projected, grads)


def pick_slots(product, slot, slot_count):
    total = jnp.zeros((RANK, product.shape[1]), jnp.float32)
    for s in range(slot_count):
        total += jnp.where(slot == s, product[s * RANK : (s + 1) * RANK], 0.0)
    return total


def exchange_kernel(
    owner,
    seq_slot_ref,
    device_jobs_ref,
    tokens_ref,
    weight_ref,
    upstream_ref,
    panels_ref,
    projected_ref,
    grads_ref,
    cols,
    tokens,
    weight,
    upstream,
    panels,
    sent_ref,
    down_ref,
    up_all,
    up_ref,
    bt,
    back,
    part_out,
    part_in,
    low,
    sums,
    frozen,
    cols_send,
    cols_recv,
    bt_send,
    bt_recv,
    back_send,
    back_recv,
    part_send,
    part_recv,
    low_send,
    low_recv,
    local_sem,
):
    count, row_count, tokens_here = cols.shape
    slot_count = bt.shape[0] // RANK
    width = tokens.shape[1]
    job_total = grads_ref.shape[0]
    half = job_total // 2
    up_start = width - owner * row_count
    up_count = row_count - up_start
    me = lax.axis_index("dp")

    group = count // 2
    seq_count = seq_slot_ref.shape[0] // count
    seq_len = tokens_here // seq_count
    low_half = me < group
    base = jnp.where(low_half, 0, group)
    place = me - base

    def peer(k):
        return lax.rem(me + k, count)

    def far(i):
        return group - base + lax.rem(place + i, group)

    def near(i):
        return base + lax.rem(place + i, group)

    def for_partners(act):
        @pl.loop(0, group)
        def _(i):
            act(far(i))

            @pl.when(i > 0)
            def _():
                act(near(i))

    def job_at(source, slot):
        return jnp.maximum(device_jobs_ref[source, slot], 0)

    def token_rows(source):
        seq = lax.broadcasted_iota(jnp.int32, (1, tokens_here), 1) // seq_len
        slot = jnp.zeros((1, tokens_here), jnp.int32)
        job = jnp.zeros((1, tokens_here), jnp.int32)
        for q in range(seq_count):
            slot_q = seq_slot_ref[source * seq_count + q]
            slot = jnp.where(seq == q, slot_q, slot)
            job = jnp.where(seq == q, job_at(source, slot_q), job)
        return slot, job

    def cols_copy(dest):
        return pltpu.make_async_remote_copy(
            src_ref=sent_ref.at[pl.ds(pl.multiple_of(dest * row_count, 16), row_count)],
            dst_ref=cols.at[me],
            send_sem=cols_send.at[dest],
            recv_sem=cols_recv.at[me],
            device_id={"dp": dest},
            device_id_type=pl.DeviceIdType.MESH,
        )

    def bt_copy(dest):
        return pltpu.make_async_remote_copy(
            src_ref=up_ref.at[dest],
            dst_ref=bt,
            send_sem=bt_send.at[dest],
            recv_sem=bt_recv,
            device_id={"dp": dest},
            device_id_type=pl.DeviceIdType.MESH,
        )

    def back_copy(dest):
        return pltpu.make_async_remote_copy(
            src_ref=back.at[me],
            dst_ref=back.at[me],
            send_sem=back_send.at[dest],
            recv_sem=back_recv.at[me],
            device_id={"dp": dest},
            device_id_type=pl.DeviceIdType.MESH,
        )

    def part_copy(dest):
        return pltpu.make_async_remote_copy(
            src_ref=part_out.at[dest],
            dst_ref=part_in.at[me],
            send_sem=part_send.at[dest],
            recv_sem=part_recv.at[me],
            device_id={"dp": dest},
            device_id_type=pl.DeviceIdType.MESH,
        )

    def low_copy():
        return pltpu.make_async_remote_copy(
            src_ref=low.at[me],
            dst_ref=low.at[me],
            send_sem=low_send,
            recv_sem=low_recv.at[me],
            device_id={"dp": owner},
            device_id_type=pl.DeviceIdType.MESH,
        )

    def arrival(buffer, sem):
        return pltpu.make_async_copy(buffer, buffer, sem)

    tokens_in = pltpu.make_async_copy(tokens_ref, tokens, local_sem.at[0])
    weight_in = pltpu.make_async_copy(weight_ref, weight, local_sem.at[1])
    upstream_in = pltpu.make_async_copy(upstream_ref, upstream, local_sem.at[2])
    panels_in = pltpu.make_async_copy(panels_ref, panels, local_sem.at[3])

    barrier = pltpu.get_barrier_semaphore()

    @pl.loop(1, count)
    def _(k):
        pl.semaphore_signal(barrier, inc=1, device_id={"dp": peer(k)}, device_id_type=pl.DeviceIdType.MESH)

    tokens_in.start()
    upstream_in.start()
    panels_in.start()
    weight_in.start()

    def split_pairs(first, last):
        @pl.loop(first, last)
        def _(pair):
            at = pl.ds(pl.multiple_of(pair * 2 * RANK, 2 * RANK), 2 * RANK)
            both = panels[:, at].astype(jnp.float32)
            even = jnp.concatenate([both[:half, :RANK], both[half:, :RANK]], axis=1)
            odd = jnp.concatenate([both[:half, RANK:], both[half:, RANK:]], axis=1)
            sums[pl.ds(2 * pair, half, stride=row_count), :] = even
            sums[pl.ds(2 * pair + 1, half, stride=row_count), :] = odd

    tokens_in.wait()
    upstream_in.wait()
    step = upstream.shape[1]

    @pl.loop(0, width // step)
    def _(i):
        at = pl.ds(pl.multiple_of(i * step, step), step)
        sent_ref[at, :] = tokens[:, at].T

    sent_ref[pl.ds(width, step), :] = upstream[...].T
    panels_in.wait()
    pl.semaphore_wait(barrier, count - 1)

    @pl.when(me == owner)
    def _():
        split_pairs(up_start // 2, row_count // 2)

        @pl.loop(0, half)
        def _(i):
            at = pl.ds(pl.multiple_of(i * row_count + up_start, 8), up_count)
            turned = sums[at, :].T.astype(up_all.dtype)
            up_all[i] = turned[:RANK]
            up_all[i + half] = turned[RANK:]

        @pl.loop(0, count)
        def _(dest):
            for s in range(slot_count):
                up_ref[dest, s * RANK : (s + 1) * RANK] = up_all[job_at(dest, s)]

        for_partners(lambda dest: bt_copy(dest).start())

    for_partners(lambda dest: cols_copy(dest).start())

    split_pairs(0, row_count // 2)
    row = me * row_count + lax.broadcasted_iota(jnp.int32, (1, row_count), 1)

    @pl.loop(0, half)
    def _(i):
        at = pl.ds(pl.multiple_of(i * row_count, 8), row_count)
        turned = jnp.where(row < width, sums[at, :].T, 0.0).astype(down_ref.dtype)
        down_ref[i] = turned[:RANK]
        down_ref[i + half] = turned[RANK:]

    sums[...] = jnp.zeros_like(sums)
    frozen[...] = jnp.zeros_like(frozen)
    weight_in.wait()
    depth = width // 8

    @pl.loop(0, 8)
    def _(i):
        at = pl.ds(pl.multiple_of(i * depth, depth), depth)
        frozen[...] += jnp.dot(tokens[:, at], weight[at, :], preferred_element_type=jnp.float32)

    cols[me] = sent_ref[pl.ds(pl.multiple_of(me * row_count, 16), row_count), :]

    @pl.when(me == owner)
    def _():
        bt[...] = up_ref[me]

    @pl.when(me != owner)
    def _():
        arrival(bt, bt_recv).wait()

    my_slot, unused = token_rows(me)
    back[me] = pick_slots(
        jnp.dot(bt[...], sent_ref[pl.ds(width, step), :], preferred_element_type=jnp.float32), my_slot, slot_count
    ).astype(back.dtype)

    for_partners(lambda dest: back_copy(dest).start())

    def lowrank_part(source):
        factor = jnp.concatenate(
            [down_ref[job_at(source, s)] for s in range(slot_count)], axis=0
        )
        product = jnp.dot(factor, cols[source], preferred_element_type=jnp.float32)
        return pick_slots(product, token_rows(source)[0], slot_count)

    def add_grads(source, right, first, rows):
        unused, job = token_rows(source)

        @pl.loop(0, half // 4)
        def _(i):
            left = cols[source, pl.ds(first, rows)]
            for tile in range(2):
                pieces = []
                for pair in range(2):
                    for upper in range(2):
                        here = job == 4 * i + 2 * tile + pair + upper * half
                        pieces.append(jnp.where(here, right, jnp.zeros_like(right)))
                product = lax.dot_general(
                    left,
                    jnp.concatenate(pieces, axis=0),
                    (((1,), (1,)), ((), ())),
                    preferred_element_type=jnp.float32,
                )
                for pair in range(2):
                    at = pl.ds(pl.multiple_of((4 * i + 2 * tile + pair) * row_count + first, 8), rows)
                    sums[at, :] += product[:, pair * 2 * RANK : (pair + 1) * 2 * RANK]

    own_part = lowrank_part(me)
    add_grads(me, back[me], 0, row_count)

    def take(source):
        arrival(cols.at[source], cols_recv.at[source]).wait()
        part_out[source] = lowrank_part(source).astype(part_out.dtype)
        part_copy(source).start()
        arrival(back.at[source], back_recv.at[source]).wait()
        add_grads(source, back[source], 0, row_count)

    @pl.loop(0, group)
    def _(i):
        take(far(group - i))

        @pl.when(i > 0)
        def _():
            take(near(group - i))

    total = own_part
    for k in range(1, count):
        source = lax.rem(me - k + count, count)
        arrival(part_in.at[source], part_recv.at[source]).wait()
        total += part_in[source].astype(jnp.float32)
    mine = total.astype(low.dtype)
    low[me] = mine

    @pl.when(me != owner)
    def _():
        low_copy().start()

    spread = jnp.concatenate(
        [jnp.where(my_slot == s, mine, jnp.zeros_like(mine)) for s in range(slot_count)], axis=0
    )
    adapted = jnp.dot(spread.T, bt[...], preferred_element_type=jnp.float32)
    projected_ref[...] = (frozen[...] + adapter_scale * adapted).astype(projected_ref.dtype)

    @pl.when(me == owner)
    def _():
        @pl.loop(0, half)
        def _(i):
            at = pl.ds(pl.multiple_of(i * row_count + up_start, 8), up_count)
            sums[at, :] = jnp.zeros((up_count, 2 * RANK), jnp.float32)

        add_grads(me, low[me], up_start, up_count)

        @pl.loop(1, count)
        def _(k):
            source = lax.rem(me - k + count, count)
            arrival(low.at[source], low_recv.at[source]).wait()
            add_grads(source, low[source], up_start, up_count)

    @pl.loop(0, row_count // 2)
    def _(pair):
        even = sums[pl.ds(2 * pair, half, stride=row_count), :]
        odd = sums[pl.ds(2 * pair + 1, half, stride=row_count), :]
        first = jnp.concatenate([even[:, :RANK], odd[:, :RANK]], axis=1)
        second = jnp.concatenate([even[:, RANK:], odd[:, RANK:]], axis=1)
        both = jnp.concatenate([first, second], axis=0) * adapter_scale
        grads_ref[:, pl.ds(pl.multiple_of(pair * 2 * RANK, 2 * RANK), 2 * RANK)] = both.astype(
            grads_ref.dtype
        )

    @pl.when(me == owner)
    def _():
        @pl.loop(1, count)
        def _(k):
            bt_copy(peer(k)).wait_send()

    @pl.when(me != owner)
    def _():
        low_copy().wait_send()

    @pl.loop(1, count)
    def _(k):
        cols_copy(peer(k)).wait_send()
        back_copy(peer(k)).wait_send()
        part_copy(peer(k)).wait_send()


def local(tokens, base_weight, panels, upstream, seq_slot, device_jobs):
    count = lax.axis_size("dp")
    tokens_here, width = tokens.shape
    head = base_weight.shape[1]
    slot_count = device_jobs.shape[1]
    job_total = panels.shape[0]
    row_count = panels.shape[1] // RANK
    owner = count - 1
    bf16 = jnp.bfloat16
    vmem = pl.BlockSpec(memory_space=pltpu.VMEM)
    smem = pl.BlockSpec(memory_space=pltpu.SMEM)
    hbm = pl.BlockSpec(memory_space=pl.ANY)
    dma = pltpu.SemaphoreType.DMA
    return pl.pallas_call(
        functools.partial(exchange_kernel, owner),
        out_shape=(
            jax.ShapeDtypeStruct((tokens_here, head), bf16),
            jax.ShapeDtypeStruct((job_total, row_count * RANK), bf16),
        ),
        in_specs=[smem, smem, hbm, hbm, hbm, hbm],
        out_specs=(vmem, vmem),
        scratch_shapes=[
            pltpu.VMEM((count, row_count, tokens_here), bf16),
            pltpu.VMEM((tokens_here, width), bf16),
            pltpu.VMEM((width, head), bf16),
            pltpu.VMEM((tokens_here, head), bf16),
            pltpu.VMEM((job_total, row_count * RANK), bf16),
            pltpu.VMEM((width + head, tokens_here), bf16),
            pltpu.VMEM((job_total, RANK, row_count), bf16),
            pltpu.VMEM((job_total, RANK, head), bf16),
            pltpu.VMEM((count, slot_count * RANK, head), bf16),
            pltpu.VMEM((slot_count * RANK, head), bf16),
            pltpu.VMEM((count, RANK, tokens_here), bf16),
            pltpu.VMEM((count, RANK, tokens_here), bf16),
            pltpu.VMEM((count, RANK, tokens_here), bf16),
            pltpu.VMEM((count, RANK, tokens_here), bf16),
            pltpu.VMEM((job_total // 2 * row_count, 2 * RANK), jnp.float32),
            pltpu.VMEM((tokens_here, head), jnp.float32),
            dma((count,)),
            dma((count,)),
            dma((count,)),
            dma,
            dma((count,)),
            dma((count,)),
            dma((count,)),
            dma((count,)),
            dma,
            dma((count,)),
            dma((4,)),
        ],
        compiler_params=pltpu.CompilerParams(
            collective_id=0, has_side_effects=True, vmem_limit_bytes=56 * 2**20
        ),
        name="exchange",
    )(seq_slot, device_jobs, tokens, base_weight, upstream, panels)


def solution(mesh):
    in_specs = (
        P(("groups", "dp"), None),
        P(),
        P("groups", "dp"),
        P(("groups", "dp"), None),
        P("groups"),
        P("groups", None),
    )
    out_specs = (P(("groups", "dp"), None), P("groups", "dp"))

    def chosen(tokens, base_weight, panels, upstream, seq_slot, device_jobs):
        width, head = base_weight.shape
        row_count = (width + head) // lax.axis_size("dp")
        fits = row_count >= head and row_count % 16 == 0 and lax.axis_size("dp") % 2 == 0 and panels.shape[0] % 32 == 0
        body = local if fits else plain_local
        return body(tokens, base_weight, panels, upstream, seq_slot, device_jobs)

    return jax.shard_map(chosen, mesh=mesh, in_specs=in_specs, out_specs=out_specs, check_vma=False)
```

```python
import functools

import jax
import jax.numpy as jnp
from jax import lax
from jax.experimental import pallas as pl
from jax.experimental.pallas import tpu as pltpu
from jax.sharding import PartitionSpec as P

RANK = 64
PAIRS = 8


adapter_scale = 0.5


def slot_panels(panels, device_jobs, rank_size):
    count = lax.axis_size("dp")
    slot_count = device_jobs.shape[1]
    chosen = jnp.take(panels, jnp.maximum(device_jobs, 0).reshape(-1), axis=0)
    outgoing = chosen.reshape(count, slot_count, panels.shape[1])
    arrived = lax.all_to_all(outgoing, "dp", split_axis=0, concat_axis=2, tiled=True)
    return arrived.reshape(slot_count, -1, rank_size)


def plain_local(tokens, base_weight, panels, upstream, seq_slot, device_jobs):
    count = lax.axis_size("dp")
    device = lax.axis_index("dp")
    width = tokens.shape[1]
    head_columns = base_weight.shape[1]
    rank_size = RANK
    seq_count = seq_slot.shape[0] // count
    seq_len = tokens.shape[0] // seq_count
    row_count = panels.shape[1] // rank_size
    job_total = panels.shape[0]
    my_slots = lax.dynamic_slice_in_dim(seq_slot, device * seq_count, seq_count)
    stacked = slot_panels(panels, device_jobs, rank_size)
    frozen_output = jnp.dot(tokens, base_weight, preferred_element_type=jnp.float32)
    seq_panels = jnp.take(stacked, my_slots, axis=0)
    adapter_down_rows = seq_panels[:, :width]
    bt_rows = seq_panels[:, width:]
    sequence_token_rows = tokens.reshape(seq_count, seq_len, width)
    seq_grads = upstream.reshape(seq_count, seq_len, head_columns)
    lowrank = jnp.einsum(
        "ovc,ocm->ovm", sequence_token_rows, adapter_down_rows, preferred_element_type=jnp.float32
    ).astype(jnp.bfloat16)
    adapted_output = jnp.einsum(
        "slr,shr->slh", lowrank, bt_rows, preferred_element_type=jnp.float32
    )
    projected = (frozen_output + adapter_scale * adapted_output.reshape(-1, head_columns)).astype(
        jnp.bfloat16
    )
    back_rank = jnp.einsum(
        "slh,shr->slr", seq_grads, bt_rows, preferred_element_type=jnp.float32
    ).astype(jnp.bfloat16)
    left = jnp.concatenate([tokens, upstream], axis=1)
    left_cols = lax.all_to_all(left, "dp", split_axis=1, concat_axis=0, tiled=True)
    right = jnp.concatenate([back_rank, lowrank], axis=2).reshape(-1, 2 * rank_size)
    right_all = lax.all_gather(right, "dp", axis=0, tiled=True)
    source = jnp.arange(count * seq_count) // seq_count
    owners = device_jobs[source, seq_slot]
    owners = jnp.where(owners < 0, job_total, owners)
    group = 16
    turns = count // group
    block_seqs = group * seq_count
    left_blocks = left_cols.reshape(turns, block_seqs, seq_len, row_count)
    right_blocks = right_all.reshape(turns, block_seqs, seq_len, 2 * rank_size)
    owner_blocks = owners.reshape(turns, block_seqs)
    first_row = device * row_count
    last_row = first_row + row_count - 1
    straddles = jnp.logical_and(first_row < width, last_row >= width)
    all_up = first_row >= width
    row_index = first_row + jnp.arange(row_count)
    down_rows = (row_index < width)[None, :, None]
    job_index = jnp.arange(job_total)

    def one_half(left_seq, right_seq):
        factor = jnp.where(all_up, right_seq[:, :, rank_size:], right_seq[:, :, :rank_size])
        return jnp.einsum("nlp,nlr->npr", left_seq, factor, preferred_element_type=jnp.float32)

    def two_halves(left_seq, right_seq):
        down_term = jnp.einsum(
            "nlp,nlr->npr",
            left_seq,
            right_seq[:, :, :rank_size],
            preferred_element_type=jnp.float32,
        )
        up_term = jnp.einsum(
            "nlp,nlr->npr",
            left_seq,
            right_seq[:, :, rank_size:],
            preferred_element_type=jnp.float32,
        )
        return jnp.where(down_rows, down_term, up_term)

    def accumulate(total_sums, item):
        left_seq, right_seq, owner_now = item
        term = lax.cond(straddles, two_halves, one_half, left_seq, right_seq)
        selector = (owner_now[:, None] == job_index[None, :]).astype(jnp.float32)
        added = jnp.dot(
            selector.T,
            term.reshape(block_seqs, -1),
            preferred_element_type=jnp.float32,
            precision=lax.Precision.HIGHEST,
        )
        return (total_sums + added, None)

    start = jnp.zeros((job_total, row_count * rank_size), jnp.float32)
    summed_output, unused = lax.scan(accumulate, start, (left_blocks, right_blocks, owner_blocks))
    grads = (adapter_scale * summed_output).astype(jnp.bfloat16)
    return (projected, grads)


def pick_slots(product, slot, slot_count):
    total = jnp.zeros((RANK, product.shape[1]), jnp.float32)
    for s in range(slot_count):
        total += jnp.where(slot == s, product[s * RANK : (s + 1) * RANK], 0.0)
    return total


def exchange_kernel(
    owner,
    seq_slot_ref,
    device_jobs_ref,
    tokens_ref,
    weight_ref,
    upstream_ref,
    panels_ref,
    projected_ref,
    grads_ref,
    cols,
    tokens,
    weight,
    upstream,
    panels,
    sent_ref,
    down_ref,
    up_all,
    up_ref,
    bt,
    back,
    part_out,
    part_in,
    low,
    sums,
    frozen,
    cols_send,
    cols_recv,
    bt_send,
    bt_recv,
    back_send,
    back_recv,
    part_send,
    part_recv,
    low_send,
    low_recv,
    local_sem,
):
    count, row_count, tokens_here = cols.shape
    slot_count = bt.shape[0] // RANK
    width = tokens.shape[1]
    job_total = grads_ref.shape[0]
    half = job_total // 2
    up_start = width - owner * row_count
    up_count = row_count - up_start
    me = lax.axis_index("dp")

    group = count // 2
    seq_count = seq_slot_ref.shape[0] // count
    seq_len = tokens_here // seq_count
    low_half = me < group
    base = jnp.where(low_half, 0, group)
    place = me - base

    def peer(k):
        return lax.rem(me + k, count)

    def far(i):
        return group - base + lax.rem(place + i, group)

    def near(i):
        return base + lax.rem(place + i, group)

    def for_partners(act):
        @pl.loop(0, group)
        def _(i):
            act(far(i))

            @pl.when(i > 0)
            def _():
                act(near(i))

    def job_at(source, slot):
        return jnp.maximum(device_jobs_ref[source, slot], 0)

    def token_rows(source):
        seq = lax.broadcasted_iota(jnp.int32, (1, tokens_here), 1) // seq_len
        slot = jnp.zeros((1, tokens_here), jnp.int32)
        job = jnp.zeros((1, tokens_here), jnp.int32)
        for q in range(seq_count):
            slot_q = seq_slot_ref[source * seq_count + q]
            slot = jnp.where(seq == q, slot_q, slot)
            job = jnp.where(seq == q, job_at(source, slot_q), job)
        return slot, job

    def cols_copy(dest):
        return pltpu.make_async_remote_copy(
            src_ref=sent_ref.at[pl.ds(pl.multiple_of(dest * row_count, 16), row_count)],
            dst_ref=cols.at[me],
            send_sem=cols_send.at[dest],
            recv_sem=cols_recv.at[me],
            device_id={"dp": dest},
            device_id_type=pl.DeviceIdType.MESH,
        )

    def bt_copy(dest):
        return pltpu.make_async_remote_copy(
            src_ref=up_ref.at[dest],
            dst_ref=bt,
            send_sem=bt_send.at[dest],
            recv_sem=bt_recv,
            device_id={"dp": dest},
            device_id_type=pl.DeviceIdType.MESH,
        )

    def back_copy(dest):
        return pltpu.make_async_remote_copy(
            src_ref=back.at[me],
            dst_ref=back.at[me],
            send_sem=back_send.at[dest],
            recv_sem=back_recv.at[me],
            device_id={"dp": dest},
            device_id_type=pl.DeviceIdType.MESH,
        )

    def part_copy(dest):
        return pltpu.make_async_remote_copy(
            src_ref=part_out.at[dest],
            dst_ref=part_in.at[me],
            send_sem=part_send.at[dest],
            recv_sem=part_recv.at[me],
            device_id={"dp": dest},
            device_id_type=pl.DeviceIdType.MESH,
        )

    def low_copy():
        return pltpu.make_async_remote_copy(
            src_ref=low.at[me],
            dst_ref=low.at[me],
            send_sem=low_send,
            recv_sem=low_recv.at[me],
            device_id={"dp": owner},
            device_id_type=pl.DeviceIdType.MESH,
        )

    def arrival(buffer, sem):
        return pltpu.make_async_copy(buffer, buffer, sem)

    tokens_in = pltpu.make_async_copy(tokens_ref, tokens, local_sem.at[0])
    weight_in = pltpu.make_async_copy(weight_ref, weight, local_sem.at[1])
    upstream_in = pltpu.make_async_copy(upstream_ref, upstream, local_sem.at[2])
    panels_in = pltpu.make_async_copy(panels_ref, panels, local_sem.at[3])

    barrier = pltpu.get_barrier_semaphore()

    @pl.loop(1, count)
    def _(k):
        pl.semaphore_signal(barrier, inc=1, device_id={"dp": peer(k)}, device_id_type=pl.DeviceIdType.MESH)

    tokens_in.start()
    upstream_in.start()
    panels_in.start()
    weight_in.start()

    def split_pairs(first, last):
        @pl.loop(first // PAIRS, last // PAIRS)
        def _(block):
            lanes = PAIRS * 2 * RANK
            at = pl.ds(pl.multiple_of(block * lanes, lanes), lanes)
            wide = panels[:, at].astype(jnp.float32)
            lines = []
            for n in range(PAIRS):
                both = wide[:, n * 2 * RANK : (n + 1) * 2 * RANK]
                lines.append(jnp.concatenate([both[:half, :RANK], both[half:, :RANK]], axis=1))
                lines.append(jnp.concatenate([both[:half, RANK:], both[half:, RANK:]], axis=1))
            for n, line in enumerate(lines):
                sums[pl.ds(block * 2 * PAIRS + n, half, stride=row_count), :] = line

    tokens_in.wait()
    upstream_in.wait()
    step = upstream.shape[1]

    @pl.loop(0, width // step, unroll=2)
    def _(i):
        at = pl.ds(pl.multiple_of(i * step, step), step)
        sent_ref[at, :] = tokens[:, at].T

    sent_ref[pl.ds(width, step), :] = upstream[...].T
    panels_in.wait()
    pl.semaphore_wait(barrier, count - 1)

    @pl.when(me == owner)
    def _():
        split_pairs(up_start // 2, row_count // 2)

        @pl.loop(0, half)
        def _(i):
            at = pl.ds(pl.multiple_of(i * row_count + up_start, 8), up_count)
            turned = sums[at, :].T.astype(up_all.dtype)
            up_all[i] = turned[:RANK]
            up_all[i + half] = turned[RANK:]

        @pl.loop(0, count)
        def _(dest):
            for s in range(slot_count):
                up_ref[dest, s * RANK : (s + 1) * RANK] = up_all[job_at(dest, s)]

        for_partners(lambda dest: bt_copy(dest).start())

    for_partners(lambda dest: cols_copy(dest).start())

    split_pairs(0, row_count // 2)
    row = me * row_count + lax.broadcasted_iota(jnp.int32, (1, row_count), 1)

    @pl.loop(0, half)
    def _(i):
        at = pl.ds(pl.multiple_of(i * row_count, 8), row_count)
        turned = jnp.where(row < width, sums[at, :].T, 0.0).astype(down_ref.dtype)
        down_ref[i] = turned[:RANK]
        down_ref[i + half] = turned[RANK:]

    sums[...] = jnp.zeros_like(sums)
    frozen[...] = jnp.zeros_like(frozen)
    weight_in.wait()
    depth = width // 8

    @pl.loop(0, 8)
    def _(i):
        at = pl.ds(pl.multiple_of(i * depth, depth), depth)
        frozen[...] += jnp.dot(tokens[:, at], weight[at, :], preferred_element_type=jnp.float32)

    cols[me] = sent_ref[pl.ds(pl.multiple_of(me * row_count, 16), row_count), :]

    @pl.when(me == owner)
    def _():
        bt[...] = up_ref[me]

    @pl.when(me != owner)
    def _():
        arrival(bt, bt_recv).wait()

    my_slot, unused = token_rows(me)
    back[me] = pick_slots(
        jnp.dot(bt[...], sent_ref[pl.ds(width, step), :], preferred_element_type=jnp.float32), my_slot, slot_count
    ).astype(back.dtype)

    for_partners(lambda dest: back_copy(dest).start())

    def lowrank_part(source):
        factor = jnp.concatenate(
            [down_ref[job_at(source, s)] for s in range(slot_count)], axis=0
        )
        product = jnp.dot(factor, cols[source], preferred_element_type=jnp.float32)
        return pick_slots(product, token_rows(source)[0], slot_count)

    def add_grads(source, right, first, rows, tiles=2):
        unused, job = token_rows(source)

        @pl.loop(0, half // (2 * tiles))
        def _(i):
            left = cols[source, pl.ds(first, rows)]
            for tile in range(tiles):
                pieces = []
                for pair in range(2):
                    for upper in range(2):
                        here = job == 2 * tiles * i + 2 * tile + pair + upper * half
                        pieces.append(jnp.where(here, right, jnp.zeros_like(right)))
                product = lax.dot_general(
                    left,
                    jnp.concatenate(pieces, axis=0),
                    (((1,), (1,)), ((), ())),
                    preferred_element_type=jnp.float32,
                )
                for pair in range(2):
                    at = pl.ds(pl.multiple_of((2 * tiles * i + 2 * tile + pair) * row_count + first, 8), rows)
                    sums[at, :] += product[:, pair * 2 * RANK : (pair + 1) * 2 * RANK]

    own_part = lowrank_part(me)
    add_grads(me, back[me], 0, row_count)

    def take(source):
        arrival(cols.at[source], cols_recv.at[source]).wait()
        part_out[source] = lowrank_part(source).astype(part_out.dtype)
        part_copy(source).start()
        arrival(back.at[source], back_recv.at[source]).wait()
        add_grads(source, back[source], 0, row_count)

    @pl.loop(0, group)
    def _(i):
        take(far(group - i))

        @pl.when(i > 0)
        def _():
            take(near(group - i))

    total = own_part
    for k in range(1, count):
        source = lax.rem(me - k + count, count)
        arrival(part_in.at[source], part_recv.at[source]).wait()
        total += part_in[source].astype(jnp.float32)
    mine = total.astype(low.dtype)
    low[me] = mine

    @pl.when(me != owner)
    def _():
        low_copy().start()

    spread = jnp.concatenate(
        [jnp.where(my_slot == s, mine, jnp.zeros_like(mine)) for s in range(slot_count)], axis=0
    )
    adapted = jnp.dot(spread.T, bt[...], preferred_element_type=jnp.float32)
    projected_ref[...] = (frozen[...] + adapter_scale * adapted).astype(projected_ref.dtype)

    @pl.when(me == owner)
    def _():
        @pl.loop(0, half)
        def _(i):
            at = pl.ds(pl.multiple_of(i * row_count + up_start, 8), up_count)
            sums[at, :] = jnp.zeros((up_count, 2 * RANK), jnp.float32)

        add_grads(me, low[me], up_start, up_count, 4)

        @pl.loop(1, count)
        def _(k):
            source = lax.rem(me - k + count, count)
            arrival(low.at[source], low_recv.at[source]).wait()
            add_grads(source, low[source], up_start, up_count, 4)

    @pl.loop(0, row_count // 2 // PAIRS)
    def _(block):
        lines = [
            sums[pl.ds(block * 2 * PAIRS + n, half, stride=row_count), :] * adapter_scale
            for n in range(2 * PAIRS)
        ]
        firsts, seconds = [], []
        for even, odd in zip(lines[::2], lines[1::2]):
            firsts.append(jnp.concatenate([even[:, :RANK], odd[:, :RANK]], axis=1))
            seconds.append(jnp.concatenate([even[:, RANK:], odd[:, RANK:]], axis=1))
        both = jnp.concatenate(
            [jnp.concatenate(firsts, axis=1), jnp.concatenate(seconds, axis=1)], axis=0
        )
        lanes = PAIRS * 2 * RANK
        grads_ref[:, pl.ds(pl.multiple_of(block * lanes, lanes), lanes)] = both.astype(grads_ref.dtype)

    @pl.when(me == owner)
    def _():
        @pl.loop(1, count)
        def _(k):
            bt_copy(peer(k)).wait_send()

    @pl.when(me != owner)
    def _():
        low_copy().wait_send()

    @pl.loop(1, count)
    def _(k):
        cols_copy(peer(k)).wait_send()
        back_copy(peer(k)).wait_send()
        part_copy(peer(k)).wait_send()


def local(tokens, base_weight, panels, upstream, seq_slot, device_jobs):
    count = lax.axis_size("dp")
    tokens_here, width = tokens.shape
    head = base_weight.shape[1]
    slot_count = device_jobs.shape[1]
    job_total = panels.shape[0]
    row_count = panels.shape[1] // RANK
    owner = count - 1
    bf16 = jnp.bfloat16
    vmem = pl.BlockSpec(memory_space=pltpu.VMEM)
    smem = pl.BlockSpec(memory_space=pltpu.SMEM)
    hbm = pl.BlockSpec(memory_space=pl.ANY)
    dma = pltpu.SemaphoreType.DMA
    return pl.pallas_call(
        functools.partial(exchange_kernel, owner),
        out_shape=(
            jax.ShapeDtypeStruct((tokens_here, head), bf16),
            jax.ShapeDtypeStruct((job_total, row_count * RANK), bf16),
        ),
        in_specs=[smem, smem, hbm, hbm, hbm, hbm],
        out_specs=(vmem, vmem),
        scratch_shapes=[
            pltpu.VMEM((count, row_count, tokens_here), bf16),
            pltpu.VMEM((tokens_here, width), bf16),
            pltpu.VMEM((width, head), bf16),
            pltpu.VMEM((tokens_here, head), bf16),
            pltpu.VMEM((job_total, row_count * RANK), bf16),
            pltpu.VMEM((width + head, tokens_here), bf16),
            pltpu.VMEM((job_total, RANK, row_count), bf16),
            pltpu.VMEM((job_total, RANK, head), bf16),
            pltpu.VMEM((count, slot_count * RANK, head), bf16),
            pltpu.VMEM((slot_count * RANK, head), bf16),
            pltpu.VMEM((count, RANK, tokens_here), bf16),
            pltpu.VMEM((count, RANK, tokens_here), bf16),
            pltpu.VMEM((count, RANK, tokens_here), bf16),
            pltpu.VMEM((count, RANK, tokens_here), bf16),
            pltpu.VMEM((job_total // 2 * row_count, 2 * RANK), jnp.float32),
            pltpu.VMEM((tokens_here, head), jnp.float32),
            dma((count,)),
            dma((count,)),
            dma((count,)),
            dma,
            dma((count,)),
            dma((count,)),
            dma((count,)),
            dma((count,)),
            dma,
            dma((count,)),
            dma((4,)),
        ],
        compiler_params=pltpu.CompilerParams(
            collective_id=0, has_side_effects=True, vmem_limit_bytes=56 * 2**20
        ),
        name="exchange",
    )(seq_slot, device_jobs, tokens, base_weight, upstream, panels)


def solution(mesh):
    in_specs = (
        P(("groups", "dp"), None),
        P(),
        P("groups", "dp"),
        P(("groups", "dp"), None),
        P("groups"),
        P("groups", None),
    )
    out_specs = (P(("groups", "dp"), None), P("groups", "dp"))

    def chosen(tokens, base_weight, panels, upstream, seq_slot, device_jobs):
        width, head = base_weight.shape
        row_count = (width + head) // lax.axis_size("dp")
        fits = row_count >= head and row_count % 16 == 0 and lax.axis_size("dp") % 2 == 0 and panels.shape[0] % 32 == 0
        body = local if fits else plain_local
        return body(tokens, base_weight, panels, upstream, seq_slot, device_jobs)

    return jax.shard_map(chosen, mesh=mesh, in_specs=in_specs, out_specs=out_specs, check_vma=False)
```

```python
import functools

import jax
import jax.numpy as jnp
from jax import lax
from jax.experimental import pallas as pl
from jax.experimental.pallas import tpu as pltpu
from jax.sharding import PartitionSpec as P

RANK = 64
PAIRS = 8


adapter_scale = 0.5


def slot_panels(panels, device_jobs, rank_size):
    count = lax.axis_size("dp")
    slot_count = device_jobs.shape[1]
    chosen = jnp.take(panels, jnp.maximum(device_jobs, 0).reshape(-1), axis=0)
    outgoing = chosen.reshape(count, slot_count, panels.shape[1])
    arrived = lax.all_to_all(outgoing, "dp", split_axis=0, concat_axis=2, tiled=True)
    return arrived.reshape(slot_count, -1, rank_size)


def plain_local(tokens, base_weight, panels, upstream, seq_slot, device_jobs):
    count = lax.axis_size("dp")
    device = lax.axis_index("dp")
    width = tokens.shape[1]
    head_columns = base_weight.shape[1]
    rank_size = RANK
    seq_count = seq_slot.shape[0] // count
    seq_len = tokens.shape[0] // seq_count
    row_count = panels.shape[1] // rank_size
    job_total = panels.shape[0]
    my_slots = lax.dynamic_slice_in_dim(seq_slot, device * seq_count, seq_count)
    stacked = slot_panels(panels, device_jobs, rank_size)
    frozen_output = jnp.dot(tokens, base_weight, preferred_element_type=jnp.float32)
    seq_panels = jnp.take(stacked, my_slots, axis=0)
    adapter_down_rows = seq_panels[:, :width]
    bt_rows = seq_panels[:, width:]
    sequence_token_rows = tokens.reshape(seq_count, seq_len, width)
    seq_grads = upstream.reshape(seq_count, seq_len, head_columns)
    lowrank = jnp.einsum(
        "ovc,ocm->ovm", sequence_token_rows, adapter_down_rows, preferred_element_type=jnp.float32
    ).astype(jnp.bfloat16)
    adapted_output = jnp.einsum(
        "slr,shr->slh", lowrank, bt_rows, preferred_element_type=jnp.float32
    )
    projected = (frozen_output + adapter_scale * adapted_output.reshape(-1, head_columns)).astype(
        jnp.bfloat16
    )
    back_rank = jnp.einsum(
        "slh,shr->slr", seq_grads, bt_rows, preferred_element_type=jnp.float32
    ).astype(jnp.bfloat16)
    left = jnp.concatenate([tokens, upstream], axis=1)
    left_cols = lax.all_to_all(left, "dp", split_axis=1, concat_axis=0, tiled=True)
    right = jnp.concatenate([back_rank, lowrank], axis=2).reshape(-1, 2 * rank_size)
    right_all = lax.all_gather(right, "dp", axis=0, tiled=True)
    source = jnp.arange(count * seq_count) // seq_count
    owners = device_jobs[source, seq_slot]
    owners = jnp.where(owners < 0, job_total, owners)
    group = 16
    turns = count // group
    block_seqs = group * seq_count
    left_blocks = left_cols.reshape(turns, block_seqs, seq_len, row_count)
    right_blocks = right_all.reshape(turns, block_seqs, seq_len, 2 * rank_size)
    owner_blocks = owners.reshape(turns, block_seqs)
    first_row = device * row_count
    last_row = first_row + row_count - 1
    straddles = jnp.logical_and(first_row < width, last_row >= width)
    all_up = first_row >= width
    row_index = first_row + jnp.arange(row_count)
    down_rows = (row_index < width)[None, :, None]
    job_index = jnp.arange(job_total)

    def one_half(left_seq, right_seq):
        factor = jnp.where(all_up, right_seq[:, :, rank_size:], right_seq[:, :, :rank_size])
        return jnp.einsum("nlp,nlr->npr", left_seq, factor, preferred_element_type=jnp.float32)

    def two_halves(left_seq, right_seq):
        down_term = jnp.einsum(
            "nlp,nlr->npr",
            left_seq,
            right_seq[:, :, :rank_size],
            preferred_element_type=jnp.float32,
        )
        up_term = jnp.einsum(
            "nlp,nlr->npr",
            left_seq,
            right_seq[:, :, rank_size:],
            preferred_element_type=jnp.float32,
        )
        return jnp.where(down_rows, down_term, up_term)

    def accumulate(total_sums, item):
        left_seq, right_seq, owner_now = item
        term = lax.cond(straddles, two_halves, one_half, left_seq, right_seq)
        selector = (owner_now[:, None] == job_index[None, :]).astype(jnp.float32)
        added = jnp.dot(
            selector.T,
            term.reshape(block_seqs, -1),
            preferred_element_type=jnp.float32,
            precision=lax.Precision.HIGHEST,
        )
        return (total_sums + added, None)

    start = jnp.zeros((job_total, row_count * rank_size), jnp.float32)
    summed_output, unused = lax.scan(accumulate, start, (left_blocks, right_blocks, owner_blocks))
    grads = (adapter_scale * summed_output).astype(jnp.bfloat16)
    return (projected, grads)


def pick_slots(product, slot, slot_count):
    total = jnp.zeros((RANK, product.shape[1]), jnp.float32)
    for s in range(slot_count):
        total += jnp.where(slot == s, product[s * RANK : (s + 1) * RANK], 0.0)
    return total


def exchange_kernel(
    owner,
    seq_slot_ref,
    device_jobs_ref,
    tokens_ref,
    weight_ref,
    upstream_ref,
    panels_ref,
    projected_ref,
    grads_ref,
    cols,
    tokens,
    weight,
    upstream,
    panels,
    sent_ref,
    down_ref,
    up_all,
    up_ref,
    bt,
    back,
    part_out,
    part_in,
    low,
    sums,
    frozen,
    cols_send,
    cols_recv,
    bt_send,
    bt_recv,
    back_send,
    back_recv,
    part_send,
    part_recv,
    low_send,
    low_recv,
    local_sem,
):
    count, row_count, tokens_here = cols.shape
    slot_count = bt.shape[0] // RANK
    width = tokens.shape[1]
    job_total = grads_ref.shape[0]
    half = job_total // 2
    up_start = width - owner * row_count
    up_count = row_count - up_start
    me = lax.axis_index("dp")

    group = count // 2
    seq_count = seq_slot_ref.shape[0] // count
    seq_len = tokens_here // seq_count
    low_half = me < group
    base = jnp.where(low_half, 0, group)
    place = me - base

    def peer(k):
        return lax.rem(me + k, count)

    def far(i):
        return group - base + lax.rem(place + i, group)

    def near(i):
        return base + lax.rem(place + i, group)

    def for_partners(act):
        @pl.loop(0, group)
        def _(i):
            act(far(i))

            @pl.when(i > 0)
            def _():
                act(near(i))

    def job_at(source, slot):
        return jnp.maximum(device_jobs_ref[source, slot], 0)

    def token_rows(source):
        seq = lax.broadcasted_iota(jnp.int32, (1, tokens_here), 1) // seq_len
        slot = jnp.zeros((1, tokens_here), jnp.int32)
        job = jnp.zeros((1, tokens_here), jnp.int32)
        for q in range(seq_count):
            slot_q = seq_slot_ref[source * seq_count + q]
            slot = jnp.where(seq == q, slot_q, slot)
            job = jnp.where(seq == q, job_at(source, slot_q), job)
        return slot, job

    def cols_copy(dest):
        return pltpu.make_async_remote_copy(
            src_ref=sent_ref.at[pl.ds(pl.multiple_of(dest * row_count, 16), row_count)],
            dst_ref=cols.at[me],
            send_sem=cols_send.at[dest],
            recv_sem=cols_recv.at[me],
            device_id={"dp": dest},
            device_id_type=pl.DeviceIdType.MESH,
        )

    def bt_copy(dest):
        return pltpu.make_async_remote_copy(
            src_ref=up_ref.at[dest],
            dst_ref=bt,
            send_sem=bt_send.at[dest],
            recv_sem=bt_recv,
            device_id={"dp": dest},
            device_id_type=pl.DeviceIdType.MESH,
        )

    def back_copy(dest):
        return pltpu.make_async_remote_copy(
            src_ref=back.at[me],
            dst_ref=back.at[me],
            send_sem=back_send.at[dest],
            recv_sem=back_recv.at[me],
            device_id={"dp": dest},
            device_id_type=pl.DeviceIdType.MESH,
        )

    def part_copy(dest):
        return pltpu.make_async_remote_copy(
            src_ref=part_out.at[dest],
            dst_ref=part_in.at[me],
            send_sem=part_send.at[dest],
            recv_sem=part_recv.at[me],
            device_id={"dp": dest},
            device_id_type=pl.DeviceIdType.MESH,
        )

    def low_copy():
        return pltpu.make_async_remote_copy(
            src_ref=low.at[me],
            dst_ref=low.at[me],
            send_sem=low_send,
            recv_sem=low_recv.at[me],
            device_id={"dp": owner},
            device_id_type=pl.DeviceIdType.MESH,
        )

    def arrival(buffer, sem):
        return pltpu.make_async_copy(buffer, buffer, sem)

    tokens_in = pltpu.make_async_copy(tokens_ref, tokens, local_sem.at[0])
    weight_in = pltpu.make_async_copy(weight_ref, weight, local_sem.at[1])
    upstream_in = pltpu.make_async_copy(upstream_ref, upstream, local_sem.at[2])
    panels_in = pltpu.make_async_copy(panels_ref, panels, local_sem.at[3])

    barrier = pltpu.get_barrier_semaphore()

    @pl.loop(1, count)
    def _(k):
        pl.semaphore_signal(barrier, inc=1, device_id={"dp": peer(k)}, device_id_type=pl.DeviceIdType.MESH)

    tokens_in.start()
    upstream_in.start()
    panels_in.start()
    weight_in.start()

    def split_pairs(first, last):
        @pl.loop(first // PAIRS, last // PAIRS)
        def _(block):
            lanes = PAIRS * 2 * RANK
            at = pl.ds(pl.multiple_of(block * lanes, lanes), lanes)
            wide = panels[:, at].astype(jnp.float32)
            lines = []
            for n in range(PAIRS):
                both = wide[:, n * 2 * RANK : (n + 1) * 2 * RANK]
                lines.append(jnp.concatenate([both[:half, :RANK], both[half:, :RANK]], axis=1))
                lines.append(jnp.concatenate([both[:half, RANK:], both[half:, RANK:]], axis=1))
            for n, line in enumerate(lines):
                sums[pl.ds(block * 2 * PAIRS + n, half, stride=row_count), :] = line

    tokens_in.wait()
    upstream_in.wait()
    step = upstream.shape[1]

    @pl.loop(0, width // step, unroll=2)
    def _(i):
        at = pl.ds(pl.multiple_of(i * step, step), step)
        sent_ref[at, :] = tokens[:, at].T

    sent_ref[pl.ds(width, step), :] = upstream[...].T
    panels_in.wait()
    pl.semaphore_wait(barrier, count - 1)

    @pl.when(me == owner)
    def _():
        split_pairs(up_start // 2, row_count // 2)

        @pl.loop(0, half)
        def _(i):
            at = pl.ds(pl.multiple_of(i * row_count + up_start, 8), up_count)
            turned = sums[at, :].T.astype(up_all.dtype)
            up_all[i] = turned[:RANK]
            up_all[i + half] = turned[RANK:]

        @pl.loop(0, count)
        def _(dest):
            for s in range(slot_count):
                up_ref[dest, s * RANK : (s + 1) * RANK] = up_all[job_at(dest, s)]

        for_partners(lambda dest: bt_copy(dest).start())

    for_partners(lambda dest: cols_copy(dest).start())

    split_pairs(0, row_count // 2)
    row = me * row_count + lax.broadcasted_iota(jnp.int32, (1, row_count), 1)

    @pl.loop(0, half)
    def _(i):
        at = pl.ds(pl.multiple_of(i * row_count, 8), row_count)
        turned = jnp.where(row < width, sums[at, :].T, 0.0).astype(down_ref.dtype)
        down_ref[i] = turned[:RANK]
        down_ref[i + half] = turned[RANK:]

    sums[...] = jnp.zeros_like(sums)
    frozen[...] = jnp.zeros_like(frozen)
    cols[me] = sent_ref[pl.ds(pl.multiple_of(me * row_count, 16), row_count), :]

    @pl.when(me == owner)
    def _():
        bt[...] = up_ref[me]

    @pl.when(me != owner)
    def _():
        arrival(bt, bt_recv).wait()

    my_slot, unused = token_rows(me)
    back[me] = pick_slots(
        jnp.dot(bt[...], sent_ref[pl.ds(width, step), :], preferred_element_type=jnp.float32), my_slot, slot_count
    ).astype(back.dtype)

    for_partners(lambda dest: back_copy(dest).start())

    weight_in.wait()
    depth = width // 8

    @pl.loop(0, 8)
    def _(i):
        at = pl.ds(pl.multiple_of(i * depth, depth), depth)
        frozen[...] += jnp.dot(tokens[:, at], weight[at, :], preferred_element_type=jnp.float32)

    def lowrank_part(source):
        factor = jnp.concatenate(
            [down_ref[job_at(source, s)] for s in range(slot_count)], axis=0
        )
        product = jnp.dot(factor, cols[source], preferred_element_type=jnp.float32)
        return pick_slots(product, token_rows(source)[0], slot_count)

    def add_grads(source, right, first, rows, tiles=4):
        unused, job = token_rows(source)

        @pl.loop(0, half // (2 * tiles))
        def _(i):
            left = cols[source, pl.ds(first, rows)]
            for tile in range(tiles):
                pieces = []
                for pair in range(2):
                    for upper in range(2):
                        here = job == 2 * tiles * i + 2 * tile + pair + upper * half
                        pieces.append(jnp.where(here, right, jnp.zeros_like(right)))
                product = lax.dot_general(
                    left,
                    jnp.concatenate(pieces, axis=0),
                    (((1,), (1,)), ((), ())),
                    preferred_element_type=jnp.float32,
                )
                for pair in range(2):
                    at = pl.ds(pl.multiple_of((2 * tiles * i + 2 * tile + pair) * row_count + first, 8), rows)
                    sums[at, :] += product[:, pair * 2 * RANK : (pair + 1) * 2 * RANK]

    own_part = lowrank_part(me)
    add_grads(me, back[me], 0, row_count)

    def take(source):
        arrival(cols.at[source], cols_recv.at[source]).wait()
        part_out[source] = lowrank_part(source).astype(part_out.dtype)
        part_copy(source).start()
        arrival(back.at[source], back_recv.at[source]).wait()
        add_grads(source, back[source], 0, row_count)

    @pl.loop(0, group)
    def _(i):
        take(far(group - i))

        @pl.when(i > 0)
        def _():
            take(near(group - i))

    total = own_part
    for k in range(1, count):
        source = lax.rem(me - k + count, count)
        arrival(part_in.at[source], part_recv.at[source]).wait()
        total += part_in[source].astype(jnp.float32)
    mine = total.astype(low.dtype)
    low[me] = mine

    @pl.when(me != owner)
    def _():
        low_copy().start()

    spread = jnp.concatenate(
        [jnp.where(my_slot == s, mine, jnp.zeros_like(mine)) for s in range(slot_count)], axis=0
    )
    adapted = jnp.dot(spread.T, bt[...], preferred_element_type=jnp.float32)
    projected_ref[...] = (frozen[...] + adapter_scale * adapted).astype(projected_ref.dtype)

    @pl.when(me == owner)
    def _():
        @pl.loop(0, half)
        def _(i):
            at = pl.ds(pl.multiple_of(i * row_count + up_start, 8), up_count)
            sums[at, :] = jnp.zeros((up_count, 2 * RANK), jnp.float32)

        add_grads(me, low[me], up_start, up_count, 4)

        @pl.loop(1, count)
        def _(k):
            source = lax.rem(me - k + count, count)
            arrival(low.at[source], low_recv.at[source]).wait()
            add_grads(source, low[source], up_start, up_count, 4)

    @pl.loop(0, row_count // 2 // PAIRS)
    def _(block):
        lines = [
            sums[pl.ds(block * 2 * PAIRS + n, half, stride=row_count), :] * adapter_scale
            for n in range(2 * PAIRS)
        ]
        firsts, seconds = [], []
        for even, odd in zip(lines[::2], lines[1::2]):
            firsts.append(jnp.concatenate([even[:, :RANK], odd[:, :RANK]], axis=1))
            seconds.append(jnp.concatenate([even[:, RANK:], odd[:, RANK:]], axis=1))
        both = jnp.concatenate(
            [jnp.concatenate(firsts, axis=1), jnp.concatenate(seconds, axis=1)], axis=0
        )
        lanes = PAIRS * 2 * RANK
        grads_ref[:, pl.ds(pl.multiple_of(block * lanes, lanes), lanes)] = both.astype(grads_ref.dtype)

    @pl.when(me == owner)
    def _():
        @pl.loop(1, count)
        def _(k):
            bt_copy(peer(k)).wait_send()

    @pl.when(me != owner)
    def _():
        low_copy().wait_send()

    @pl.loop(1, count)
    def _(k):
        cols_copy(peer(k)).wait_send()
        back_copy(peer(k)).wait_send()
        part_copy(peer(k)).wait_send()


def local(tokens, base_weight, panels, upstream, seq_slot, device_jobs):
    count = lax.axis_size("dp")
    tokens_here, width = tokens.shape
    head = base_weight.shape[1]
    slot_count = device_jobs.shape[1]
    job_total = panels.shape[0]
    row_count = panels.shape[1] // RANK
    owner = count - 1
    bf16 = jnp.bfloat16
    vmem = pl.BlockSpec(memory_space=pltpu.VMEM)
    smem = pl.BlockSpec(memory_space=pltpu.SMEM)
    hbm = pl.BlockSpec(memory_space=pl.ANY)
    dma = pltpu.SemaphoreType.DMA
    return pl.pallas_call(
        functools.partial(exchange_kernel, owner),
        out_shape=(
            jax.ShapeDtypeStruct((tokens_here, head), bf16),
            jax.ShapeDtypeStruct((job_total, row_count * RANK), bf16),
        ),
        in_specs=[smem, smem, hbm, hbm, hbm, hbm],
        out_specs=(vmem, vmem),
        scratch_shapes=[
            pltpu.VMEM((count, row_count, tokens_here), bf16),
            pltpu.VMEM((tokens_here, width), bf16),
            pltpu.VMEM((width, head), bf16),
            pltpu.VMEM((tokens_here, head), bf16),
            pltpu.VMEM((job_total, row_count * RANK), bf16),
            pltpu.VMEM((width + head, tokens_here), bf16),
            pltpu.VMEM((job_total, RANK, row_count), bf16),
            pltpu.VMEM((job_total, RANK, head), bf16),
            pltpu.VMEM((count, slot_count * RANK, head), bf16),
            pltpu.VMEM((slot_count * RANK, head), bf16),
            pltpu.VMEM((count, RANK, tokens_here), bf16),
            pltpu.VMEM((count, RANK, tokens_here), bf16),
            pltpu.VMEM((count, RANK, tokens_here), bf16),
            pltpu.VMEM((count, RANK, tokens_here), bf16),
            pltpu.VMEM((job_total // 2 * row_count, 2 * RANK), jnp.float32),
            pltpu.VMEM((tokens_here, head), jnp.float32),
            dma((count,)),
            dma((count,)),
            dma((count,)),
            dma,
            dma((count,)),
            dma((count,)),
            dma((count,)),
            dma((count,)),
            dma,
            dma((count,)),
            dma((4,)),
        ],
        compiler_params=pltpu.CompilerParams(
            collective_id=0, has_side_effects=True, vmem_limit_bytes=56 * 2**20
        ),
        name="exchange",
    )(seq_slot, device_jobs, tokens, base_weight, upstream, panels)


def solution(mesh):
    in_specs = (
        P(("groups", "dp"), None),
        P(),
        P("groups", "dp"),
        P(("groups", "dp"), None),
        P("groups"),
        P("groups", None),
    )
    out_specs = (P(("groups", "dp"), None), P("groups", "dp"))

    def chosen(tokens, base_weight, panels, upstream, seq_slot, device_jobs):
        width, head = base_weight.shape
        row_count = (width + head) // lax.axis_size("dp")
        fits = row_count >= head and row_count % 16 == 0 and lax.axis_size("dp") % 2 == 0 and panels.shape[0] % 32 == 0
        body = local if fits else plain_local
        return body(tokens, base_weight, panels, upstream, seq_slot, device_jobs)

    return jax.shard_map(chosen, mesh=mesh, in_specs=in_specs, out_specs=out_specs, check_vma=False)
```
